32 devices in a mesh: seq: 8 (over z, y), tr: 2 (over x), tc: 2 (over core).
Axes of the slice: x: 2, y: 2, z: 4, core: 2. Of those that a mesh axis runs over, the one named last changes fastest.
Arguments:
- activations: bfloat16 [8192, 1024], P('seq', ('tr', 'tc')), may hold values from -6 to 6
- seg_len: int32 [8], P('seq'), may hold values from 1 to 1024, as said below
- seg_start: int32 [8], P('seq'), may hold values from 0 to 1, as said below
- memory_rates: float32 [3, 8, 8], P(None, 'seq'), may hold values from 0 to 1, as said below
- w_qkv: bfloat16 [1024, 3, 1024], P(None, None, ('tr', 'tc')), may hold values from -0.1875 to 0.1875
- conv_w: float32 [4, 3, 1024], P(None, None, ('tr', 'tc')), may hold values from -3 to 3
- persistent: bfloat16 [2, 16, 1024], P(None, None, ('tr', 'tc')), may hold values from -6 to 6
- w_out: bfloat16 [1024, 1024], P(('tr', 'tc')), may hold values from -0.1875 to 0.1875
- w_gate: bfloat16 [1024, 2816], P(None, ('tr', 'tc')), may hold values from -0.1875 to 0.1875
- w_up: bfloat16 [1024, 2816], P(None, ('tr', 'tc')), may hold values from -0.1875 to 0.1875
- w_down: bfloat16 [2816, 1024], P(('tr', 'tc')), may hold values from -0.109375 to 0.109375
Outputs:
- layer_out: bfloat16 [8192, 1024], P('seq', ('tr', 'tc'))
The draws below stay inside these ranges and needn't reach their ends.
Inputs may be any that keep to these rules, and one draw needn't show every extreme that they name: `seg_start`: 1 where a segment begins a prompt, 0 where it continues the prompt of the segment before; segment 0 begins a prompt; a prompt spans at most 4 segments, and in every draw one prompt spans exactly that many. `seg_len`: live tokens at the head of each segment; every segment of a prompt but its last is full. `memory_rates`: all three tables lie strictly between 0 and 1.
All inputs are finite; a program needn't handle non-finite values.
Results may differ from the reference program's by a relative error of at most 0.015.
Values may be sent and summed in bfloat16 or wider, within the bound.
A program may use at most 192 MiB of HBM per device.

```python
import math
import jax
import jax.numpy as jnp
from jax import lax

D = 1024
MEMORY_HEADS = 8
HD = 128
FF = 2816
SEG = 1024
PERSIST = 16
CONV = 4
SEGMENT_TOTAL = 8
TOKENS = 8192
TGROUPS = 4


def segment_tables(key):
    base = jax.random.fold_in(key, 11)
    key_coin, key_place, key_fill = jax.random.split(base, 3)
    longest = SEGMENT_TOTAL // 2
    index = jnp.arange(SEGMENT_TOTAL, dtype=jnp.int32)
    coin = jax.random.randint(key_coin, (SEGMENT_TOTAL,), 0, 10) < 3
    begins = coin | (index % longest == 0)
    anchor = jax.random.randint(key_place, (), 0, SEGMENT_TOTAL - longest + 1)
    inside = (index > anchor) & (index < anchor + longest)
    begins = jnp.where(inside, False, begins) | (index == anchor) | (index == anchor + longest)
    starts = begins.astype(jnp.int32)
    follows = jnp.concatenate([starts[1:], jnp.ones((1,), jnp.int32)])
    partial_len = jax.random.randint(key_fill, (SEGMENT_TOTAL,), 1, SEG + 1)
    lengths = jnp.where(follows == 1, partial_len, SEG).astype(jnp.int32)
    return (starts, lengths)


def draw_seg_start(key, part):
    return segment_tables(key)[0]


def draw_seg_len(key, part):
    return segment_tables(key)[1]


def draw_memory_rates(key, part):
    key_rows = jax.random.split(jax.random.fold_in(key, 23), 9)
    fast_share = 0.5
    slow_low = 0.003
    slow_high = 0.015
    theta = jnp.exp(jax.random.uniform(key_rows[7], (SEGMENT_TOTAL, MEMORY_HEADS), jnp.float32, math.log(0.002), math.log(0.01)))
    fast = jax.random.uniform(key_rows[0], (MEMORY_HEADS,)) < fast_share
    fast_rate = jnp.exp(jax.random.uniform(key_rows[1], (MEMORY_HEADS,), jnp.float32, math.log(0.25), math.log(0.55)))
    slow_rate = jnp.exp(jax.random.uniform(key_rows[2], (MEMORY_HEADS,), jnp.float32, math.log(slow_low), math.log(slow_high)))
    baseline_rate = jnp.where(fast, fast_rate, slow_rate)
    random_noise = jnp.exp(jax.random.uniform(key_rows[3], (SEGMENT_TOTAL, MEMORY_HEADS), jnp.float32, math.log(0.6), math.log(1.6)))
    compelled_flag = jax.random.randint(key_rows[8], (), 0, SEGMENT_TOTAL)
    spike_event = (jax.random.uniform(key_rows[4], (SEGMENT_TOTAL, 1)) < 0.06) | (jnp.arange(SEGMENT_TOTAL)[:, None] == compelled_flag)
    spike_rate = jax.random.uniform(key_rows[5], (SEGMENT_TOTAL, MEMORY_HEADS), jnp.float32, 0.2, 0.5)
    decay_factor = jnp.where(spike_event, jnp.maximum(baseline_rate * random_noise, spike_rate), baseline_rate * random_noise)
    eta = jax.random.uniform(key_rows[6], (SEGMENT_TOTAL, MEMORY_HEADS), jnp.float32, 0.3, 0.8)
    return jnp.stack([decay_factor, eta, theta]).astype(jnp.float32)


def levels(rng, dims, cuts, least, top_value):
    def one(dim, shards_of):
        steps = jax.random.uniform(jax.random.fold_in(jax.random.fold_in(rng, 6), dim), (shards_of,), jnp.float32, least / len(cuts), top_value / len(cuts))
        return jnp.repeat(jnp.exp(steps), dims[dim] // shards_of).reshape((-1,) + (1,) * (len(dims) - dim - 1))

    factor_of = one(*cuts[0])
    for cut in cuts[1:]:
        factor_of = factor_of * one(*cut)
    return factor_of


def noise(stream_key, shape, scale, most, shards=(), kind=jnp.bfloat16):
    entries = scale * jax.random.normal(stream_key, shape, jnp.float32)
    if shards:
        entries = entries * levels(stream_key, shape, shards, -0.22, 0.18)
    return jnp.clip(entries, -most, most).astype(kind)


def setup_inputs(seed: int = 0) -> dict:
    arg_keys = jax.random.split(jax.random.key(seed), 12)
    return {
        "activations": noise(arg_keys[0], (TOKENS, D), 1.0, 6.0, ((0, 8), (1, 4))),
        "seg_len": draw_seg_len(jax.random.fold_in(arg_keys[11], 71), 0),
        "seg_start": draw_seg_start(jax.random.fold_in(arg_keys[11], 71), 0),
        "memory_rates": draw_memory_rates(jax.random.fold_in(arg_keys[11], 71), 0),
        "w_qkv": noise(arg_keys[4], (D, 3, MEMORY_HEADS * HD), D ** -0.5, 0.1875, ((2, 4),)),
        "conv_w": noise(arg_keys[5], (CONV, 3, MEMORY_HEADS * HD), 0.5, 3.0, ((2, 4),), jnp.float32),
        "persistent": noise(arg_keys[6], (2, PERSIST, MEMORY_HEADS * HD), 1.0, 6.0, ((2, 4),)),
        "w_out": noise(arg_keys[7], (MEMORY_HEADS * HD, D), (MEMORY_HEADS * HD) ** -0.5, 0.1875, ((0, 4),)),
        "w_gate": noise(arg_keys[8], (D, FF), D ** -0.5, 0.1875, ((1, 4),)),
        "w_up": noise(arg_keys[9], (D, FF), D ** -0.5, 0.1875, ((1, 4),)),
        "w_down": noise(arg_keys[10], (FF, D), FF ** -0.5, 0.109375, ((0, 4),)),
    }


epsilon = 1e-06
score_scale = 8.0

def unit_rows(values_in):
    return values_in * lax.rsqrt(lax.optimization_barrier(jnp.sum(values_in * values_in, -1, keepdims=True)) + epsilon)

def reference(activations, seg_len, seg_start, memory_rates, w_qkv, conv_w, persistent, w_out, w_gate, w_up, w_down):
    width = MEMORY_HEADS * HD
    wide = w_qkv.reshape(D, 3 * width)
    taps = conv_w.reshape(CONV, 3 * width).astype(jnp.float32)
    position = jnp.arange(SEG, dtype=jnp.int32)
    x_segs = activations.reshape(SEGMENT_TOTAL, SEG, D)

    def project(x_seg):
        xf = x_seg.astype(jnp.float32)
        inv_rms = lax.rsqrt(lax.optimization_barrier(jnp.sum(xf * xf, -1)) / D + epsilon)
        return (jnp.dot(x_seg, wide, preferred_element_type=jnp.float32) * inv_rms[:, None]).astype(jnp.bfloat16)
    qkv_segs = lax.map(project, x_segs)
    tails = qkv_segs[:, SEG - (CONV - 1):]
    before = jnp.concatenate([jnp.zeros((1, CONV - 1, 3 * width), jnp.bfloat16), tails[:-1]], 0)

    def convolve(inputs):
        qkv_seg, edge_rows, start_flag = inputs
        extended = jnp.concatenate([edge_rows, qkv_seg], 0)
        continuing = start_flag == 0
        total = jnp.zeros((SEG, 3 * width), jnp.float32)
        for offset in range(CONV):
            shifted = extended[CONV - 1 - offset:CONV - 1 - offset + SEG].astype(jnp.float32)
            valid = (position >= offset) | continuing
            total = total + jnp.where(valid[:, None], taps[offset] * shifted, 0.0)
        parts = total.reshape(SEG, 3, MEMORY_HEADS, HD)
        query_n = unit_rows(parts[:, 0]).astype(jnp.bfloat16)
        key_n = unit_rows(parts[:, 1]).astype(jnp.bfloat16)
        value_n = parts[:, 2].astype(jnp.bfloat16)
        return (query_n, key_n, value_n)
    qn, kn, values = lax.map(convolve, (qkv_segs, before, seg_start))
    pkeys = unit_rows(persistent[0].astype(jnp.float32).reshape(PERSIST, MEMORY_HEADS, HD)).astype(jnp.bfloat16)
    pvalues = persistent[1].reshape(PERSIST, MEMORY_HEADS, HD)
    live = position[None, :] < seg_len[:, None]
    keys_live = jnp.where(live[:, :, None, None], kn, jnp.zeros((), jnp.bfloat16))
    a_mats = jnp.einsum('cthi,cthj->chij', keys_live.astype(jnp.float32), keys_live.astype(jnp.float32))
    b_mats = jnp.einsum('cthi,cthj->chij', keys_live.astype(jnp.float32), values.astype(jnp.float32))
    rates = jnp.transpose(memory_rates, (1, 0, 2))

    def memory_step(carry, inputs):
        memory, momentum = carry
        query_seg, a_mat, b_mat, rate_row, start_flag = inputs
        keep = (1 - start_flag).astype(jnp.float32)
        memory_in = memory * keep
        momentum_in = momentum * keep
        retr = jnp.einsum('thi,hij->thj', query_seg.astype(jnp.float32), memory_in, precision=lax.Precision.HIGHEST)
        decay_factor = rate_row[0][:, None, None]
        eta = rate_row[1][:, None, None]
        theta = rate_row[2][:, None, None]
        grad = jnp.matmul(a_mat, memory_in, precision=lax.Precision.HIGHEST) - b_mat
        momentum_out = eta * momentum_in - theta * grad
        memory_out = (1.0 - decay_factor) * memory_in + momentum_out
        return ((memory_out, momentum_out), retr)
    zero_state = jnp.zeros((MEMORY_HEADS, HD, HD), jnp.float32)
    _, retr = lax.scan(memory_step, (zero_state, zero_state), (qn, a_mats, b_mats, rates, seg_start))
    mem = retr * lax.rsqrt(lax.optimization_barrier(jnp.mean(retr * retr, -1, keepdims=True)) + epsilon)

    def attend(inputs):
        query_seg, key_seg, value_seg, length = inputs
        keys_all = jnp.concatenate([pkeys, key_seg], 0).astype(jnp.float32)
        values_all = jnp.concatenate([pvalues, value_seg], 0).astype(jnp.float32)
        scores = score_scale * jnp.einsum('qhd,khd->hqk', query_seg.astype(jnp.float32), keys_all)
        rows_q = position[:, None]
        cols_k = jnp.arange(PERSIST + SEG, dtype=jnp.int32)[None, :] - PERSIST
        allow = (cols_k < 0) | (cols_k <= rows_q) & (cols_k < length)
        weights = jnp.where(allow[None], jnp.exp(scores), 0.0)
        probs = (weights / lax.optimization_barrier(jnp.sum(weights, -1, keepdims=True))).astype(jnp.bfloat16)
        return jnp.einsum('hqk,khd->qhd', probs.astype(jnp.float32), values_all)
    attn = lax.map(attend, (qn, kn, values, seg_len))
    heads_out = (attn + mem).astype(jnp.bfloat16).reshape(SEGMENT_TOTAL, SEG, width)
    group_heads = width // TGROUPS
    group_units = FF // TGROUPS

    def finish(inputs):
        x_seg, out_seg = inputs
        proj = jnp.zeros((SEG, D), jnp.float32)
        for group in range(TGROUPS):
            term = jnp.dot(out_seg[:, group * group_heads:(group + 1) * group_heads], w_out[group * group_heads:(group + 1) * group_heads], preferred_element_type=jnp.float32).astype(jnp.bfloat16)
            term = lax.optimization_barrier(term)
            proj = proj + term.astype(jnp.float32)
        resid = (x_seg.astype(jnp.float32) + proj).astype(jnp.bfloat16)
        resid_f = resid.astype(jnp.float32)
        inv_rms2 = lax.rsqrt(lax.optimization_barrier(jnp.sum(resid_f * resid_f, -1)) / D + epsilon)
        gate = jnp.dot(resid, w_gate, preferred_element_type=jnp.float32) * inv_rms2[:, None]
        up = jnp.dot(resid, w_up, preferred_element_type=jnp.float32) * inv_rms2[:, None]
        hidden = (jax.nn.silu(gate) * up).astype(jnp.bfloat16)
        ffn = jnp.zeros((SEG, D), jnp.float32)
        for group in range(TGROUPS):
            term = jnp.dot(hidden[:, group * group_units:(group + 1) * group_units], w_down[group * group_units:(group + 1) * group_units], preferred_element_type=jnp.float32).astype(jnp.bfloat16)
            term = lax.optimization_barrier(term)
            ffn = ffn + term.astype(jnp.float32)
        return (resid_f + ffn).astype(jnp.bfloat16)
    layer_out = lax.map(finish, (x_segs, heads_out))
    return layer_out.reshape(TOKENS, D)
```

```python
import functools

import jax
import jax.numpy as jnp
from jax import lax
from jax.experimental import pallas as pl
from jax.experimental.pallas import tpu as pltpu
from jax.sharding import PartitionSpec as P

HD = 128
SEG = 1024
CONV = 4
NC = 4
CR = SEG // NC
EPS = 1e-06
MESH = pl.DeviceIdType.MESH
F32 = jnp.float32
BF16 = jnp.bfloat16


def mm(a, b):
    return jnp.dot(a, b, preferred_element_type=F32)


def mm_t(a, b):
    return lax.dot_general(a, b, (((1,), (1,)), ((), ())), preferred_element_type=F32)


def unit_rows(v):
    return v * lax.rsqrt(jnp.sum(v * v, -1, keepdims=True) + EPS)


def split2(v):
    hi = v.astype(BF16)
    return hi, (v - hi.astype(F32)).astype(BF16)


def kernel(
    n_seq,
    span,
    len_ref,
    start_ref,
    rates_ref,
    x_ref,
    wqkv_ref,
    conv_ref,
    pers_ref,
    wout_ref,
    wgate_ref,
    wup_ref,
    wdown_ref,
    out_ref,
    xg,
    ext,
    edge_out,
    edge_in,
    qb,
    kb,
    va,
    pkb,
    pva,
    attn,
    packet,
    states,
    wog,
    hog,
    resid0,
    part0,
    part2,
    rs1_out,
    rs1_in,
    rs2_out,
    rs2_in,
    xs_s, xs_r, xx_s, xx_r, xf_s, xf_r,
    ws_s, ws_r,
    hs_s, hs_r, hx_s, hx_r, hf_s, hf_r,
    ed_s, ed_r,
    st_s, st_r,
    r1_s, r1_r, r2_s, r2_r,
):
    seq, tr, tc = lax.axis_index("seq"), lax.axis_index("tr"), lax.axis_index("tc")
    sib = (seq, tr, 1 - tc)
    xnb = (seq, 1 - tr, tc)
    d_model = 4 * 256
    group = (tr * 2 + tc, tr * 2 + 1 - tc, (1 - tr) * 2 + tc, (1 - tr) * 2 + 1 - tc)
    cols = [pl.ds(pl.multiple_of(g * 256, 256), 256) for g in group]

    def ahead(d):
        return (lax.rem(seq + d, n_seq), tr, tc)

    def send(src, dst, ssem, rsem, dev):
        return pltpu.make_async_remote_copy(
            src_ref=src, dst_ref=dst, send_sem=ssem, recv_sem=rsem, device_id=dev, device_id_type=MESH
        )

    barrier = pltpu.get_barrier_semaphore()
    peers = [sib, xnb] + [ahead(d) for d in range(1, span)] + [ahead(n_seq - d) for d in range(1, span)]
    for peer in peers:
        pl.semaphore_signal(barrier, inc=1, device_id=peer, device_id_type=MESH)
    pl.semaphore_wait(barrier, len(peers))

    def x_sib(c):
        return send(x_ref.at[c], xg.at[0, c], xs_s.at[c], xs_r.at[c], sib)

    def x_xnb(c):
        return send(x_ref.at[c], xg.at[1, c], xx_s.at[c], xx_r.at[c], xnb)

    def x_fwd(c):
        return send(xg.at[1, c], xg.at[2, c], xf_s.at[c], xf_r.at[c], sib)

    def h_sib(c):
        return send(hog.at[0, c], hog.at[1, c], hs_s.at[c], hs_r.at[c], sib)

    def h_xnb(c):
        return send(hog.at[0, c], hog.at[2, c], hx_s.at[c], hx_r.at[c], xnb)

    def h_fwd(c):
        return send(hog.at[2, c], hog.at[3, c], hf_s.at[c], hf_r.at[c], sib)

    def rs1(c):
        return send(rs1_out.at[c], rs1_in.at[c], r1_s.at[c], r1_r.at[c], sib)

    def rs2(c):
        return send(rs2_out.at[c], rs2_in.at[c], r2_s.at[c], r2_r.at[c], xnb)

    w_sib = send(wout_ref, wog.at[0], ws_s.at[0], ws_r.at[0], sib)
    w_xnb = send(wout_ref, wog.at[1], ws_s.at[1], ws_r.at[1], xnb)
    w_fwd = send(wog.at[1], wog.at[2], ws_s.at[2], ws_r.at[2], sib)
    edge = send(edge_out, edge_in, ed_s, ed_r, ahead(1))

    def state(d):
        return send(packet, states.at[d - 1], st_s.at[d - 1], st_r.at[d - 1], ahead(d))

    order = (NC - 1,) + tuple(range(NC - 1))
    for c in order:
        x_xnb(c).start()
        x_sib(c).start()

    length = len_ref[0]
    continuing = start_ref[0] == 0
    keep = jnp.where(continuing, 1.0, 0.0).astype(F32)

    pkb[...] = jnp.zeros_like(pkb)
    pva[...] = jnp.zeros_like(pva)
    for h in range(2):
        lanes = slice(h * HD, (h + 1) * HD)
        pkb[h, 0:16, :] = unit_rows(pers_ref[0, :, lanes].astype(F32)).astype(BF16)
        pva[h, 0:16, 0:HD] = pers_ref[1, :, lanes]
        pva[h, 0:16, HD:] = jnp.ones((16, HD), BF16)

    def wq(t):
        return wqkv_ref[pl.ds(pl.multiple_of(group[t] * 256, 256), 256), :]

    def rows8(c):
        return pl.ds(pl.multiple_of(8 + c * CR, 8), CR)

    def first_half(i, _):
        c = lax.rem(i + NC - 1, NC)
        x_sib(c).wait_recv()
        ext[rows8(c), :] = mm(x_ref[c], wq(0)) + mm(xg[0, c], wq(1))
        return 0

    lax.fori_loop(0, NC, first_half, 0)

    def sumsq(v):
        v = v.astype(F32)
        return jnp.sum(v * v, -1, keepdims=True)

    def second_half(i, _):
        c = lax.rem(i + NC - 1, NC)
        x_xnb(c).wait_recv()
        x_fwd(c).start()
        acc = ext[rows8(c), :] + mm(xg[1, c], wq(2))
        sq = sumsq(x_ref[c]) + sumsq(xg[0, c]) + sumsq(xg[1, c])
        x_fwd(c).wait_recv()
        acc = acc + mm(xg[2, c], wq(3))
        sq = sq + sumsq(xg[2, c])
        qkv = (acc * lax.rsqrt(sq / d_model + EPS)).astype(BF16).astype(F32)
        ext[rows8(c), :] = qkv

        @pl.when(i == 0)
        def _():
            edge_out[...] = qkv[CR - 8 :, :]
            edge.start()

        return 0

    lax.fori_loop(0, NC, second_half, 0)
    w_xnb.start()
    w_sib.start()

    def conv_chunk(c):
        r0 = pl.multiple_of(c * CR, CR)
        live = (lax.broadcasted_iota(jnp.int32, (CR, HD), 0) + r0) < length
        for p in range(3):
            for h in range(2):
                lanes = slice(h * HD, (h + 1) * HD)
                slab = ext[pl.ds(r0, CR + 8), p * 256 + h * HD : p * 256 + (h + 1) * HD]
                total = jnp.zeros((CR, HD), F32)
                for j in range(CONV):
                    total = total + conv_ref[j, p : p + 1, lanes] * slab[8 - j : 8 - j + CR, :]
                if p == 0:
                    qb[h, pl.ds(r0, CR), :] = unit_rows(total).astype(BF16)
                elif p == 1:
                    kb[h, pl.ds(r0, CR), :] = jnp.where(live, unit_rows(total), 0.0).astype(BF16)
                else:
                    va[h, pl.ds(r0, CR), 0:HD] = jnp.where(live, total, 0.0).astype(BF16)
                    va[h, pl.ds(r0, CR), HD:] = jnp.where(live, 1.0, 0.0).astype(BF16)

    def conv_step(i, _):
        conv_chunk(i + 1)
        return 0

    lax.fori_loop(0, NC - 1, conv_step, 0)
    edge.wait_recv()
    ext[0:8, :] = edge_in[...] * keep
    conv_chunk(0)

    row = lax.broadcasted_iota(jnp.int32, (16, 256), 0)
    for h in range(2):
        head = group[0] * 2 + h
        alpha, eta, theta = rates_ref[0, 0, head], rates_ref[1, 0, head], rates_ref[2, 0, head]
        kh = kb[h]
        a_mat = lax.dot_general(kh, kh, (((0,), (0,)), ((), ())), preferred_element_type=F32)
        b_mat = lax.dot_general(
            kh, va[h, :, 0:HD], (((0,), (0,)), ((), ())), preferred_element_type=F32
        )
        packet[h, 0:HD, 0:HD] = (a_mat * (theta * keep)).astype(BF16)
        packet[h, 0:HD, HD:] = (b_mat * theta).astype(BF16)
        d_hi, d_lo = split2(jnp.full((16, 256), (1.0 - alpha) * keep, F32))
        e_hi, e_lo = split2(jnp.full((16, 256), eta * keep, F32))
        pick = jnp.where(row == 0, d_hi.astype(F32), jnp.where(row == 1, d_lo.astype(F32), 0.0))
        pick = jnp.where(row == 2, e_hi.astype(F32), jnp.where(row == 3, e_lo.astype(F32), pick))
        packet[h, HD : HD + 16, :] = pick.astype(BF16)
    for d in range(1, span):
        state(d).start()

    tri = lax.broadcasted_iota(jnp.int32, (CR, CR), 1) <= lax.broadcasted_iota(jnp.int32, (CR, CR), 0)
    for c in range(NC):
        for h in range(2):
            q8 = qb[h, c * CR : (c + 1) * CR, :] * 8
            pv = mm(jnp.exp(mm_t(q8, pkb[h])).astype(BF16), pva[h])
            if c:
                w = jnp.exp(mm_t(q8, kb[h, 0 : c * CR, :])).astype(BF16)
                pv = pv + mm(w, va[h, 0 : c * CR, :])
            w = jnp.where(tri, jnp.exp(mm_t(q8, kb[h, c * CR : (c + 1) * CR, :])), 0.0)
            pv = pv + mm(w.astype(BF16), va[h, c * CR : (c + 1) * CR, :])
            attn[h, c * CR : (c + 1) * CR, :] = pv[:, :HD] / pv[:, HD:]

    w_xnb.wait_recv()
    w_fwd.start()

    def chain(i, carry):
        d = span - 1 - i
        state(d).wait_recv()
        new = []
        for h in range(2):
            mem, mom = carry[2 * h], carry[2 * h + 1]
            scal = states[d - 1, h, HD : HD + 16, 0:HD].astype(F32)
            dec, eta = scal[0:1] + scal[1:2], scal[2:3] + scal[3:4]
            hi, lo = split2(mem)
            a_mat = states[d - 1, h, 0:HD, 0:HD]
            mom = eta * mom - (mm(a_mat, hi) + mm(a_mat, lo)) + states[d - 1, h, 0:HD, HD:].astype(F32)
            new += [dec * mem + mom, mom]
        return tuple(new)

    zero = jnp.zeros((HD, HD), F32)
    carry = (zero, zero, zero, zero)
    if span <= 4:
        for i in range(span - 1):
            carry = chain(i, carry)
    else:
        carry = lax.fori_loop(0, span - 1, chain, carry)
    mats = [split2(carry[2 * h] * keep) for h in range(2)]

    for c in range(NC):
        for h in range(2):
            qh = qb[h, c * CR : (c + 1) * CR, :]
            retr = mm(qh, mats[h][0]) + mm(qh, mats[h][1])
            mem = retr * lax.rsqrt(jnp.mean(retr * retr, -1, keepdims=True) + EPS)
            hog[0, c, :, h * HD : (h + 1) * HD] = (
                attn[h, c * CR : (c + 1) * CR, :] + mem
            ).astype(BF16)
        h_xnb(c).start()
        h_sib(c).start()

    w_sib.wait_recv()
    w_fwd.wait_recv()

    def wo(s, t):
        return wout_ref[:, cols[t]] if s == 0 else wog[s - 1, :, cols[t]]

    def wrows(ref, t):
        return ref[cols[t], :]

    def reduce_x(c):
        rs1(c).wait_recv()
        rs2_out[c] = (part2[c] + rs1_in[c, 1].astype(F32)).astype(BF16)
        rs2(c).start()
        part0[c] = part0[c] + rs1_in[c, 0].astype(F32)

    def ffn(c, _):
        h_xnb(c).wait_recv()
        h_fwd(c).start()
        h_sib(c).wait_recv()
        h0, h1, h2 = hog[0, c], hog[1, c], hog[2, c]
        accs = [mm(h0, wo(0, t)) + mm(h1, wo(1, t)) + mm(h2, wo(2, t)) for t in range(4)]
        h_fwd(c).wait_recv()
        h3 = hog[3, c]
        res = []
        sq = jnp.zeros((CR, 1), F32)
        for t in range(4):
            xt = x_ref[c] if t == 0 else xg[t - 1, c]
            r = (xt.astype(F32) + (accs[t] + mm(h3, wo(3, t)))).astype(BF16)
            sq = sq + sumsq(r)
            res.append(r)
        resid0[...] = res[0].astype(F32)
        inv = lax.rsqrt(sq / d_model + EPS)

        @pl.when(c > 0)
        def _():
            reduce_x(c - 1)

        gate = sum(mm(res[t], wrows(wgate_ref, t)) for t in range(4)) * inv
        up = sum(mm(res[t], wrows(wup_ref, t)) for t in range(4)) * inv
        hidden = (gate / (1.0 + jnp.exp(-gate)) * up).astype(BF16)
        rs1_out[c, 0] = mm(hidden, wdown_ref[:, cols[1]]).astype(BF16)
        rs1_out[c, 1] = mm(hidden, wdown_ref[:, cols[3]]).astype(BF16)
        rs1(c).start()
        part2[c] = mm(hidden, wdown_ref[:, cols[2]])
        part0[c] = mm(hidden, wdown_ref[:, cols[0]]) + resid0[...]
        return 0

    lax.fori_loop(0, NC, ffn, 0)
    reduce_x(NC - 1)

    def last(c, _):
        rs2(c).wait_recv()
        out_ref[c] = (part0[c] + rs2_in[c].astype(F32)).astype(BF16)
        return 0

    lax.fori_loop(0, NC, last, 0)

    def drain(c, _):
        for copy in (x_sib, x_xnb, x_fwd, h_sib, h_xnb, h_fwd, rs1, rs2):
            copy(c).wait_send()
        return 0

    lax.fori_loop(0, NC, drain, 0)
    w_sib.wait_send()
    w_xnb.wait_send()
    w_fwd.wait_send()
    edge.wait_send()
    for d in range(1, span):
        state(d).wait_send()


def body(n_seq, activations, seg_len, seg_start, memory_rates, w_qkv, conv_w, persistent, w_out, w_gate, w_up, w_down):
    span = n_seq // 2
    full = w_qkv.shape[0]
    hw = w_qkv.shape[2]
    ff = w_gate.shape[1]
    vmem = pl.BlockSpec(memory_space=pltpu.VMEM)
    smem = pl.BlockSpec(memory_space=pltpu.SMEM)
    dma = pltpu.SemaphoreType.DMA
    per_chunk = dma((NC,))
    out = pl.pallas_call(
        functools.partial(kernel, n_seq, span),
        out_shape=jax.ShapeDtypeStruct((NC, CR, hw), BF16),
        in_specs=[smem, smem, smem] + [vmem] * 8,
        out_specs=vmem,
        scratch_shapes=[
            pltpu.VMEM((3, NC, CR, hw), BF16),
            pltpu.VMEM((SEG + 8, 3 * hw), F32),
            pltpu.VMEM((8, 3 * hw), F32),
            pltpu.VMEM((8, 3 * hw), F32),
            pltpu.VMEM((2, SEG, HD), BF16),
            pltpu.VMEM((2, SEG, HD), BF16),
            pltpu.VMEM((2, SEG, 2 * HD), BF16),
            pltpu.VMEM((2, HD, HD), BF16),
            pltpu.VMEM((2, HD, 2 * HD), BF16),
            pltpu.VMEM((2, SEG, HD), F32),
            pltpu.VMEM((2, HD + 16, 2 * HD), BF16),
            pltpu.VMEM((span - 1, 2, HD + 16, 2 * HD), BF16),
            pltpu.VMEM((3, hw, full), BF16),
            pltpu.VMEM((4, NC, CR, hw), BF16),
            pltpu.VMEM((CR, hw), F32),
            pltpu.VMEM((NC, CR, hw), F32),
            pltpu.VMEM((NC, CR, hw), F32),
            pltpu.VMEM((NC, 2, CR, hw), BF16),
            pltpu.VMEM((NC, 2, CR, hw), BF16),
            pltpu.VMEM((NC, CR, hw), BF16),
            pltpu.VMEM((NC, CR, hw), BF16),
        ]
        + [per_chunk] * 6
        + [dma((3,))] * 2
        + [per_chunk] * 6
        + [dma, dma]
        + [dma((span - 1,))] * 2
        + [per_chunk] * 4,
        compiler_params=pltpu.CompilerParams(
            collective_id=0, has_side_effects=True, vmem_limit_bytes=56 * 1024 * 1024
        ),
    )(
        seg_len,
        seg_start,
        memory_rates,
        activations.reshape(NC, CR, hw),
        w_qkv.reshape(full, 3 * hw),
        conv_w,
        persistent,
        w_out,
        w_gate,
        w_up,
        w_down,
    )
    return out.reshape(SEG, hw)


def solution(mesh):
    return jax.shard_map(
        functools.partial(body, mesh.shape["seq"]),
        mesh=mesh,
        in_specs=(
            P("seq", ("tr", "tc")),
            P("seq"),
            P("seq"),
            P(None, "seq", None),
            P(None, None, ("tr", "tc")),
            P(None, None, ("tr", "tc")),
            P(None, None, ("tr", "tc")),
            P(("tr", "tc"), None),
            P(None, ("tr", "tc")),
            P(None, ("tr", "tc")),
            P(("tr", "tc"), None),
        ),
        out_specs=P("seq", ("tr", "tc")),
        check_vma=False,
    )
```

```python
import functools

import jax
import jax.numpy as jnp
from jax import lax
from jax.experimental import pallas as pl
from jax.experimental.pallas import tpu as pltpu
from jax.sharding import PartitionSpec as P

HD = 128
SEG = 1024
CONV = 4
NC = 4
CR = SEG // NC
EPS = 1e-06
MESH = pl.DeviceIdType.MESH
F32 = jnp.float32
BF16 = jnp.bfloat16


def mm(a, b):
    return jnp.dot(a, b, preferred_element_type=F32)


def mm_t(a, b):
    return lax.dot_general(a, b, (((1,), (1,)), ((), ())), preferred_element_type=F32)


def unit_rows(v):
    return v * lax.rsqrt(jnp.sum(v * v, -1, keepdims=True) + EPS)


def split2(v):
    hi = v.astype(BF16)
    return hi, (v - hi.astype(F32)).astype(BF16)


def kernel(
    n_seq,
    span,
    len_ref,
    start_ref,
    rates_ref,
    x_hbm,
    wqkv_hbm,
    conv_ref,
    pers_ref,
    wout_hbm,
    wgate_hbm,
    wup_hbm,
    wdown_hbm,
    out_ref,
    xg,
    wqkv_ref,
    wgate_ref,
    wup_ref,
    wdown_ref,
    ext,
    edge_out,
    edge_in,
    qb,
    kb,
    va,
    pkb,
    pva,
    attn,
    ab,
    packet,
    states,
    wog,
    hog,
    resid0,
    part0,
    part2,
    rs1_out,
    rs1_in,
    rs2_out,
    rs2_in,
    xs_s, xs_r, xx_s, xx_r, xf_s, xf_r,
    ws_s, ws_r,
    hs_s, hs_r, hx_s, hx_r, hf_s, hf_r,
    ed_s, ed_r,
    st_s, st_r,
    r1_s, r1_r, r2_s, r2_r,
    lc_s,
):
    seq, tr, tc = lax.axis_index("seq"), lax.axis_index("tr"), lax.axis_index("tc")
    sib = (seq, tr, 1 - tc)
    xnb = (seq, 1 - tr, tc)
    d_model = 4 * 256
    group = (tr * 2 + tc, tr * 2 + 1 - tc, (1 - tr) * 2 + tc, (1 - tr) * 2 + 1 - tc)
    cols = [pl.ds(pl.multiple_of(g * 256, 256), 256) for g in group]

    def ahead(d):
        return (lax.rem(seq + d, n_seq), tr, tc)

    def send(src, dst, ssem, rsem, dev):
        return pltpu.make_async_remote_copy(
            src_ref=src, dst_ref=dst, send_sem=ssem, recv_sem=rsem, device_id=dev, device_id_type=MESH
        )

    fetches = [
        pltpu.make_async_copy(src, dst, lc_s.at[i])
        for i, (src, dst) in enumerate(
            (
                (x_hbm, xg.at[0]),
                (wqkv_hbm, wqkv_ref),
                (wout_hbm, wog.at[0]),
                (wgate_hbm, wgate_ref),
                (wup_hbm, wup_ref),
                (wdown_hbm, wdown_ref),
            )
        )
    ]
    for fetch in fetches:
        fetch.start()

    barrier = pltpu.get_barrier_semaphore()
    peers = [sib, xnb] + [ahead(d) for d in range(1, span)] + [ahead(n_seq - d) for d in range(1, span)]
    for peer in peers:
        pl.semaphore_signal(barrier, inc=1, device_id=peer, device_id_type=MESH)
    pl.semaphore_wait(barrier, len(peers))

    def x_sib(c):
        return send(x_hbm.at[c], xg.at[1, c], xs_s.at[c], xs_r.at[c], sib)

    def x_xnb(c):
        return send(x_hbm.at[c], xg.at[2, c], xx_s.at[c], xx_r.at[c], xnb)

    def x_fwd(c):
        return send(xg.at[2, c], xg.at[3, c], xf_s.at[c], xf_r.at[c], sib)

    def h_sib(c):
        return send(hog.at[0, c], hog.at[1, c], hs_s.at[c], hs_r.at[c], sib)

    def h_xnb(c):
        return send(hog.at[0, c], hog.at[2, c], hx_s.at[c], hx_r.at[c], xnb)

    def h_fwd(c):
        return send(hog.at[2, c], hog.at[3, c], hf_s.at[c], hf_r.at[c], sib)

    def rs1(c):
        return send(rs1_out.at[c], rs1_in.at[c], r1_s.at[c], r1_r.at[c], sib)

    def rs2(c):
        return send(rs2_out.at[c], rs2_in.at[c], r2_s.at[c], r2_r.at[c], xnb)

    w_sib = send(wog.at[0], wog.at[1], ws_s.at[0], ws_r.at[0], sib)
    w_xnb = send(wog.at[0], wog.at[2], ws_s.at[1], ws_r.at[1], xnb)
    w_fwd = send(wog.at[2], wog.at[3], ws_s.at[2], ws_r.at[2], sib)
    edge = send(edge_out, edge_in, ed_s, ed_r, ahead(1))

    def state(d):
        return send(packet, states.at[d - 1], st_s.at[d - 1], st_r.at[d - 1], ahead(d))

    order = (NC - 1,) + tuple(range(NC - 1))
    for c in order:
        x_xnb(c).start()
        x_sib(c).start()

    length = len_ref[0]
    continuing = start_ref[0] == 0
    keep = jnp.where(continuing, 1.0, 0.0).astype(F32)

    pkb[...] = jnp.zeros_like(pkb)
    pva[...] = jnp.zeros_like(pva)
    for h in range(2):
        lanes = slice(h * HD, (h + 1) * HD)
        pkb[h, 0:16, :] = unit_rows(pers_ref[0, :, lanes].astype(F32)).astype(BF16)
        pva[h, 0:16, 0:HD] = pers_ref[1, :, lanes]
        pva[h, 0:16, HD:] = jnp.ones((16, HD), BF16)

    def project(c, pair):
        lhs = [xg[t, c] for t in pair]
        return [
            sum(mm(x, wqkv_ref[p, cols[t], :]) for x, t in zip(lhs, pair)) for p in range(3)
        ]

    def rows8(c):
        return slice(8 + c * CR, 8 + (c + 1) * CR)

    fetches[0].wait()
    fetches[1].wait()
    for c in order:
        x_sib(c).wait_recv()
        for p, part in enumerate(project(c, (0, 1))):
            ext[rows8(c), p * 256 : (p + 1) * 256] = part

    def sumsq(v):
        v = v.astype(F32)
        return jnp.sum(v * v, -1, keepdims=True)

    def finish_projection(c):
        x_xnb(c).wait_recv()
        x_fwd(c).start()
        sq = sumsq(xg[0, c]) + sumsq(xg[1, c]) + sumsq(xg[2, c])
        x_fwd(c).wait_recv()
        inv = lax.rsqrt((sq + sumsq(xg[3, c])) / d_model + EPS)
        for p, part in enumerate(project(c, (2, 3))):
            lanes = slice(p * 256, (p + 1) * 256)
            ext[rows8(c), lanes] = ((ext[rows8(c), lanes] + part) * inv).astype(BF16).astype(F32)

    def conv_chunk(c):
        rows = slice(c * CR, (c + 1) * CR)
        live = (lax.broadcasted_iota(jnp.int32, (CR, HD), 0) + c * CR) < length
        for p in range(3):
            for h in range(2):
                lanes = slice(h * HD, (h + 1) * HD)
                slab = ext[c * CR : (c + 1) * CR + 8, p * 256 + h * HD : p * 256 + (h + 1) * HD]
                total = jnp.zeros((CR, HD), F32)
                for j in range(CONV):
                    total = total + conv_ref[p, j : j + 1, lanes] * slab[8 - j : 8 - j + CR, :]
                if p == 0:
                    qb[h, rows, :] = unit_rows(total).astype(BF16)
                elif p == 1:
                    kb[h, rows, :] = jnp.where(live, unit_rows(total), 0.0).astype(BF16)
                else:
                    va[h, rows, 0:HD] = jnp.where(live, total, 0.0).astype(BF16)
                    va[h, rows, HD:] = jnp.where(live, 1.0, 0.0).astype(BF16)
        for h in range(2):
            kh = kb[h, rows, :]
            both = jnp.concatenate([kh, va[h, rows, 0:HD]], 1)
            term = lax.dot_general(kh, both, (((0,), (0,)), ((), ())), preferred_element_type=F32)
            ab[h] = term if c == 0 else ab[h] + term

    finish_projection(NC - 1)
    edge_out[...] = ext[SEG : SEG + 8, :]
    edge.start()
    finish_projection(0)
    edge.wait_recv()
    ext[0:8, :] = edge_in[...] * keep
    conv_chunk(0)
    for c in range(1, NC - 1):
        finish_projection(c)
        if c == NC - 2:
            fetches[2].wait()
            w_xnb.start()
            w_sib.start()
        conv_chunk(c)
    conv_chunk(NC - 1)

    row = lax.broadcasted_iota(jnp.int32, (16, 256), 0)
    for h in range(2):
        head = group[0] * 2 + h
        alpha, eta, theta = rates_ref[0, 0, head], rates_ref[1, 0, head], rates_ref[2, 0, head]
        packet[h, 0:HD, 0:HD] = (ab[h, :, 0:HD] * (theta * keep)).astype(BF16)
        packet[h, 0:HD, HD:] = (ab[h, :, HD:] * theta).astype(BF16)
        d_hi, d_lo = split2(jnp.full((16, 256), (1.0 - alpha) * keep, F32))
        e_hi, e_lo = split2(jnp.full((16, 256), eta * keep, F32))
        pick = jnp.where(row == 0, d_hi.astype(F32), jnp.where(row == 1, d_lo.astype(F32), 0.0))
        pick = jnp.where(row == 2, e_hi.astype(F32), jnp.where(row == 3, e_lo.astype(F32), pick))
        packet[h, HD : HD + 16, :] = pick.astype(BF16)
    for d in range(span - 1, 0, -1):
        state(d).start()

    tri = lax.broadcasted_iota(jnp.int32, (CR, CR), 1) <= lax.broadcasted_iota(jnp.int32, (CR, CR), 0)
    for c in range(NC):
        for h in range(2):
            q8 = qb[h, c * CR : (c + 1) * CR, :] * 8
            pv = mm(jnp.exp(mm_t(q8, pkb[h])).astype(BF16), pva[h])
            if c:
                w = jnp.exp(mm_t(q8, kb[h, 0 : c * CR, :])).astype(BF16)
                pv = pv + mm(w, va[h, 0 : c * CR, :])
            w = jnp.where(tri, jnp.exp(mm_t(q8, kb[h, c * CR : (c + 1) * CR, :])), 0.0)
            pv = pv + mm(w.astype(BF16), va[h, c * CR : (c + 1) * CR, :])
            attn[h, c * CR : (c + 1) * CR, :] = pv[:, :HD] / pv[:, HD:]

    w_xnb.wait_recv()
    w_fwd.start()

    def chain(i, carry):
        d = span - 1 - i
        state(d).wait_recv()
        new = []
        for h in range(2):
            mem, mom = carry[2 * h], carry[2 * h + 1]
            scal = states[d - 1, h, HD : HD + 16, 0:HD].astype(F32)
            dec, eta = scal[0:1] + scal[1:2], scal[2:3] + scal[3:4]
            hi, lo = split2(mem)
            a_mat = states[d - 1, h, 0:HD, 0:HD]
            mom = eta * mom - (mm(a_mat, hi) + mm(a_mat, lo)) + states[d - 1, h, 0:HD, HD:].astype(F32)
            new += [dec * mem + mom, mom]
        return tuple(new)

    zero = jnp.zeros((HD, HD), F32)
    carry = (zero, zero, zero, zero)
    if span <= 4:
        for i in range(span - 1):
            carry = chain(i, carry)
    else:
        carry = lax.fori_loop(0, span - 1, chain, carry)
    mats = [split2(carry[2 * h] * keep) for h in range(2)]

    for c in range(NC):
        for h in range(2):
            qh = qb[h, c * CR : (c + 1) * CR, :]
            retr = mm(qh, mats[h][0]) + mm(qh, mats[h][1])
            mem = retr * lax.rsqrt(jnp.mean(retr * retr, -1, keepdims=True) + EPS)
            hog[0, c, :, h * HD : (h + 1) * HD] = (
                attn[h, c * CR : (c + 1) * CR, :] + mem
            ).astype(BF16)
        h_xnb(c).start()
        h_sib(c).start()

    w_sib.wait_recv()
    w_fwd.wait_recv()
    for fetch in fetches[3:]:
        fetch.wait()

    def wo(s, t):
        return wog[s, :, cols[t]]

    def wrows(ref, t):
        return ref[:, cols[t]]

    def reduce_x(c):
        rs1(c).wait_recv()
        rs2_out[c] = (part2[c] + rs1_in[c, 1].astype(F32)).astype(BF16)
        rs2(c).start()
        part0[c] = part0[c] + rs1_in[c, 0].astype(F32)

    def ffn(c, _):
        h_xnb(c).wait_recv()
        h_fwd(c).start()
        h_sib(c).wait_recv()
        h0, h1, h2 = hog[0, c], hog[1, c], hog[2, c]
        accs = [mm(h0, wo(0, t)) + mm(h1, wo(1, t)) + mm(h2, wo(2, t)) for t in range(4)]
        h_fwd(c).wait_recv()
        h3 = hog[3, c]
        res = []
        sq = jnp.zeros((CR, 1), F32)
        for t in range(4):
            r = (xg[t, c].astype(F32) + (accs[t] + mm(h3, wo(3, t)))).astype(BF16)
            sq = sq + sumsq(r)
            res.append(r)
        resid0[...] = res[0].astype(F32)
        inv = lax.rsqrt(sq / d_model + EPS)

        @pl.when(c > 0)
        def _():
            reduce_x(c - 1)

        gate = sum(mm_t(res[t], wrows(wgate_ref, t)) for t in range(4)) * inv
        up = sum(mm_t(res[t], wrows(wup_ref, t)) for t in range(4)) * inv
        hidden = (gate / (1.0 + jnp.exp(-gate)) * up).astype(BF16)
        rs1_out[c, 0] = mm(hidden, wdown_ref[:, cols[1]]).astype(BF16)
        rs1_out[c, 1] = mm(hidden, wdown_ref[:, cols[3]]).astype(BF16)
        rs1(c).start()
        part2[c] = mm(hidden, wdown_ref[:, cols[2]])
        part0[c] = mm(hidden, wdown_ref[:, cols[0]]) + resid0[...]
        return 0

    lax.fori_loop(0, NC, ffn, 0)
    reduce_x(NC - 1)

    def last(c, _):
        rs2(c).wait_recv()
        out_ref[c] = (part0[c] + rs2_in[c].astype(F32)).astype(BF16)
        return 0

    lax.fori_loop(0, NC, last, 0)

    def drain(c, _):
        for copy in (x_sib, x_xnb, x_fwd, h_sib, h_xnb, h_fwd, rs1, rs2):
            copy(c).wait_send()
        return 0

    lax.fori_loop(0, NC, drain, 0)
    w_sib.wait_send()
    w_xnb.wait_send()
    w_fwd.wait_send()
    edge.wait_send()
    for d in range(1, span):
        state(d).wait_send()


def body(n_seq, activations, seg_len, seg_start, memory_rates, w_qkv, conv_w, persistent, w_out, w_gate, w_up, w_down):
    span = n_seq // 2
    full = w_qkv.shape[0]
    hw = w_qkv.shape[2]
    ff = w_gate.shape[1]
    vmem = pl.BlockSpec(memory_space=pltpu.VMEM)
    hbm = pl.BlockSpec(memory_space=pl.ANY)
    smem = pl.BlockSpec(memory_space=pltpu.SMEM)
    dma = pltpu.SemaphoreType.DMA
    per_chunk = dma((NC,))
    out = pl.pallas_call(
        functools.partial(kernel, n_seq, span),
        out_shape=jax.ShapeDtypeStruct((NC, CR, hw), BF16),
        in_specs=[smem, smem, smem, hbm, hbm, vmem, vmem] + [hbm] * 4,
        out_specs=vmem,
        scratch_shapes=[
            pltpu.VMEM((4, NC, CR, hw), BF16),
            pltpu.VMEM((3, full, hw), BF16),
            pltpu.VMEM((ff, full), BF16),
            pltpu.VMEM((ff, full), BF16),
            pltpu.VMEM((ff, full), BF16),
            pltpu.VMEM((SEG + 8, 3 * hw), F32),
            pltpu.VMEM((8, 3 * hw), F32),
            pltpu.VMEM((8, 3 * hw), F32),
            pltpu.VMEM((2, SEG, HD), BF16),
            pltpu.VMEM((2, SEG, HD), BF16),
            pltpu.VMEM((2, SEG, 2 * HD), BF16),
            pltpu.VMEM((2, HD, HD), BF16),
            pltpu.VMEM((2, HD, 2 * HD), BF16),
            pltpu.VMEM((2, SEG, HD), F32),
            pltpu.VMEM((2, HD, 2 * HD), F32),
            pltpu.VMEM((2, HD + 16, 2 * HD), BF16),
            pltpu.VMEM((span - 1, 2, HD + 16, 2 * HD), BF16),
            pltpu.VMEM((4, hw, full), BF16),
            pltpu.VMEM((4, NC, CR, hw), BF16),
            pltpu.VMEM((CR, hw), F32),
            pltpu.VMEM((NC, CR, hw), F32),
            pltpu.VMEM((NC, CR, hw), F32),
            pltpu.VMEM((NC, 2, CR, hw), BF16),
            pltpu.VMEM((NC, 2, CR, hw), BF16),
            pltpu.VMEM((NC, CR, hw), BF16),
            pltpu.VMEM((NC, CR, hw), BF16),
        ]
        + [per_chunk] * 6
        + [dma((3,))] * 2
        + [per_chunk] * 6
        + [dma, dma]
        + [dma((span - 1,))] * 2
        + [per_chunk] * 4
        + [dma((6,))],
        compiler_params=pltpu.CompilerParams(
            collective_id=0, has_side_effects=True, vmem_limit_bytes=56 * 1024 * 1024
        ),
    )(
        seg_len,
        seg_start,
        memory_rates,
        activations.reshape(NC, CR, hw),
        jnp.transpose(w_qkv, (1, 0, 2)),
        jnp.transpose(conv_w, (1, 0, 2)),
        persistent,
        w_out,
        w_gate.T,
        w_up.T,
        w_down,
    )
    return out.reshape(SEG, hw)


def solution(mesh):
    return jax.shard_map(
        functools.partial(body, mesh.shape["seq"]),
        mesh=mesh,
        in_specs=(
            P("seq", ("tr", "tc")),
            P("seq"),
            P("seq"),
            P(None, "seq", None),
            P(None, None, ("tr", "tc")),
            P(None, None, ("tr", "tc")),
            P(None, None, ("tr", "tc")),
            P(("tr", "tc"), None),
            P(None, ("tr", "tc")),
            P(None, ("tr", "tc")),
            P(("tr", "tc"), None),
        ),
        out_specs=P("seq", ("tr", "tc")),
        check_vma=False,
    )
```

```python
import functools

import jax
import jax.numpy as jnp
from jax import lax
from jax.experimental import pallas as pl
from jax.experimental.pallas import tpu as pltpu
from jax.sharding import PartitionSpec as P

HD = 128
SEG = 1024
CONV = 4
NC = 4
CR = SEG // NC
EPS = 1e-06
MESH = pl.DeviceIdType.MESH
F32 = jnp.float32
BF16 = jnp.bfloat16


def mm(a, b):
    return jnp.dot(a, b, preferred_element_type=F32)


def mm_t(a, b):
    return lax.dot_general(a, b, (((1,), (1,)), ((), ())), preferred_element_type=F32)


def unit_rows(v):
    return v * lax.rsqrt(jnp.sum(v * v, -1, keepdims=True) + EPS)


def split2(v):
    hi = v.astype(BF16)
    return hi, (v - hi.astype(F32)).astype(BF16)


def kernel(
    n_seq,
    span,
    len_ref,
    start_ref,
    rates_ref,
    x_hbm,
    wqkv_hbm,
    conv_ref,
    pers_ref,
    wout_hbm,
    wgate_hbm,
    wup_hbm,
    wdown_hbm,
    out_ref,
    xg,
    wqkv_ref,
    wgate_ref,
    wup_ref,
    wdown_ref,
    ext,
    edge_out,
    edge_in,
    qb,
    kb,
    va,
    pkb,
    pva,
    attn,
    ab,
    pk_a,
    pk_b,
    st_a,
    st_b,
    mid_out,
    mid_in,
    projb,
    resb,
    wog,
    hog,
    part0,
    part2,
    rs1_out,
    rs1_in,
    rs2_out,
    rs2_in,
    xs_s, xs_r, xx_s, xx_r, xf_s, xf_r,
    ws_s, ws_r,
    hs_s, hs_r, hx_s, hx_r, hf_s, hf_r,
    ed_s, ed_r,
    sa_s, sa_r,
    sb_s, sb_r,
    md_s, md_r,
    r1_s, r1_r, r2_s, r2_r,
    lc_s,
):
    seq, tr, tc = lax.axis_index("seq"), lax.axis_index("tr"), lax.axis_index("tc")
    sib = (seq, tr, 1 - tc)
    xnb = (seq, 1 - tr, tc)
    d_model = 4 * 256
    group = (tr * 2 + tc, tr * 2 + 1 - tc, (1 - tr) * 2 + tc, (1 - tr) * 2 + 1 - tc)
    cols = [pl.ds(pl.multiple_of(g * 256, 256), 256) for g in group]

    def ahead(d):
        return (lax.rem(seq + d, n_seq), tr, tc)

    def send(src, dst, ssem, rsem, dev):
        return pltpu.make_async_remote_copy(
            src_ref=src, dst_ref=dst, send_sem=ssem, recv_sem=rsem, device_id=dev, device_id_type=MESH
        )

    fetches = [
        pltpu.make_async_copy(src, dst, lc_s.at[i])
        for i, (src, dst) in enumerate(
            (
                (x_hbm, xg.at[0]),
                (wqkv_hbm, wqkv_ref),
                (wout_hbm, wog.at[0]),
                (wgate_hbm, wgate_ref),
                (wup_hbm, wup_ref),
                (wdown_hbm, wdown_ref),
            )
        )
    ]
    for fetch in fetches:
        fetch.start()

    short = span == 4
    reach = 3 if short else span
    direct = 2 if short else span
    barrier = pltpu.get_barrier_semaphore()
    peers = [sib, xnb] + [ahead(d) for d in range(1, reach)] + [ahead(n_seq - d) for d in range(1, reach)]
    for peer in peers:
        pl.semaphore_signal(barrier, inc=1, device_id=peer, device_id_type=MESH)
    pl.semaphore_wait(barrier, len(peers))

    def x_sib(c):
        return send(x_hbm.at[c], xg.at[1, c], xs_s.at[c], xs_r.at[c], sib)

    def x_xnb(c):
        return send(x_hbm.at[c], xg.at[2, c], xx_s.at[c], xx_r.at[c], xnb)

    def x_fwd(c):
        return send(xg.at[2, c], xg.at[3, c], xf_s.at[c], xf_r.at[c], sib)

    def h_sib(c):
        return send(hog.at[0, c], hog.at[1, c], hs_s.at[c], hs_r.at[c], sib)

    def h_xnb(c):
        return send(hog.at[0, c], hog.at[2, c], hx_s.at[c], hx_r.at[c], xnb)

    def h_fwd(c):
        return send(hog.at[2, c], hog.at[3, c], hf_s.at[c], hf_r.at[c], sib)

    def rs1(c):
        return send(rs1_out.at[c], rs1_in.at[c], r1_s.at[c], r1_r.at[c], sib)

    def rs2(c):
        return send(rs2_out.at[c], rs2_in.at[c], r2_s.at[c], r2_r.at[c], xnb)

    w_sib = send(wog.at[0], wog.at[1], ws_s.at[0], ws_r.at[0], sib)
    w_xnb = send(wog.at[0], wog.at[2], ws_s.at[1], ws_r.at[1], xnb)
    w_fwd = send(wog.at[2], wog.at[3], ws_s.at[2], ws_r.at[2], sib)
    edge = send(edge_out, edge_in, ed_s, ed_r, ahead(1))

    def map_a(d):
        return send(pk_a, st_a.at[d - 1], sa_s.at[d - 1], sa_r.at[d - 1], ahead(d))

    def map_b(d):
        return send(pk_b, st_b.at[d - 1], sb_s.at[d - 1], sb_r.at[d - 1], ahead(d))

    middle = send(mid_out, mid_in, md_s, md_r, ahead(2)) if short else None

    order = (NC - 1,) + tuple(range(NC - 1))
    for c in order:
        x_xnb(c).start()
        x_sib(c).start()

    length = len_ref[0]
    continuing = start_ref[0] == 0
    keep = jnp.where(continuing, 1.0, 0.0).astype(F32)

    pkb[...] = jnp.zeros_like(pkb)
    pva[...] = jnp.zeros_like(pva)
    for h in range(2):
        lanes = slice(h * HD, (h + 1) * HD)
        pkb[h, 0:16, :] = unit_rows(pers_ref[0, :, lanes].astype(F32)).astype(BF16)
        pva[h, 0:16, 0:HD] = pers_ref[1, :, lanes]
        pva[h, 0:16, HD:] = jnp.ones((16, HD), BF16)

    def project(c, pair):
        lhs = [xg[t, c] for t in pair]
        return [
            sum(mm(x, wqkv_ref[p, cols[t], :]) for x, t in zip(lhs, pair)) for p in range(3)
        ]

    def rows8(c):
        return slice(8 + c * CR, 8 + (c + 1) * CR)

    fetches[0].wait()
    fetches[1].wait()
    for c in order:
        x_sib(c).wait_recv()
        for p, part in enumerate(project(c, (0, 1))):
            ext[rows8(c), p * 256 : (p + 1) * 256] = part

    def sumsq(v):
        v = v.astype(F32)
        return jnp.sum(v * v, -1, keepdims=True)

    def finish_projection(c):
        x_xnb(c).wait_recv()
        x_fwd(c).start()
        sq = sumsq(xg[0, c]) + sumsq(xg[1, c]) + sumsq(xg[2, c])
        x_fwd(c).wait_recv()
        inv = lax.rsqrt((sq + sumsq(xg[3, c])) / d_model + EPS)
        for p, part in enumerate(project(c, (2, 3))):
            lanes = slice(p * 256, (p + 1) * 256)
            ext[rows8(c), lanes] = ((ext[rows8(c), lanes] + part) * inv).astype(BF16).astype(F32)

    def conv_chunk(c):
        rows = slice(c * CR, (c + 1) * CR)
        live = (lax.broadcasted_iota(jnp.int32, (CR, HD), 0) + c * CR) < length
        for p in range(3):
            for h in range(2):
                lanes = slice(h * HD, (h + 1) * HD)
                slab = ext[c * CR : (c + 1) * CR + 8, p * 256 + h * HD : p * 256 + (h + 1) * HD]
                total = jnp.zeros((CR, HD), F32)
                for j in range(CONV):
                    total = total + conv_ref[p, j : j + 1, lanes] * slab[8 - j : 8 - j + CR, :]
                if p == 0:
                    qb[h, rows, :] = unit_rows(total).astype(BF16)
                elif p == 1:
                    kb[h, rows, :] = jnp.where(live, unit_rows(total), 0.0).astype(BF16)
                else:
                    va[h, rows, 0:HD] = jnp.where(live, total, 0.0).astype(BF16)
                    va[h, rows, HD:] = jnp.where(live, 1.0, 0.0).astype(BF16)
        for h in range(2):
            kh = kb[h, rows, :]
            both = jnp.concatenate([kh, va[h, rows, 0:HD]], 1)
            term = lax.dot_general(kh, both, (((0,), (0,)), ((), ())), preferred_element_type=F32)
            ab[h] = term if c == 0 else ab[h] + term

    finish_projection(NC - 1)
    edge_out[...] = ext[SEG : SEG + 8, :]
    edge.start()
    finish_projection(0)
    edge.wait_recv()
    ext[0:8, :] = edge_in[...] * keep
    conv_chunk(0)
    for c in range(1, NC - 1):
        finish_projection(c)
        if c == NC - 2:
            fetches[2].wait()
            w_xnb.start()
            w_sib.start()
        conv_chunk(c)
    conv_chunk(NC - 1)

    row = lax.broadcasted_iota(jnp.int32, (16, HD), 0)
    rates = [[rates_ref[k, 0, group[0] * 2 + h] for k in range(3)] for h in range(2)]
    for h in range(2):
        pk_b[h] = (ab[h, :, HD:] * rates[h][2]).astype(BF16)
    for d in range(direct - 1, 0, -1):
        map_b(d).start()
    for h in range(2):
        alpha, eta, theta = rates[h]
        pk_a[h, 0:HD, :] = (ab[h, :, 0:HD] * (theta * keep)).astype(BF16)
        d_hi, d_lo = split2(jnp.full((16, HD), (1.0 - alpha) * keep, F32))
        e_hi, e_lo = split2(jnp.full((16, HD), eta * keep, F32))
        pick = jnp.where(row == 0, d_hi.astype(F32), jnp.where(row == 1, d_lo.astype(F32), 0.0))
        pick = jnp.where(row == 2, e_hi.astype(F32), jnp.where(row == 3, e_lo.astype(F32), pick))
        pk_a[h, HD : HD + 16, :] = pick.astype(BF16)
    for d in range(direct - 1, 0, -1):
        map_a(d).start()

    def advance(mem, mom, a_ref, b_ref, h):
        scal = a_ref[h, HD : HD + 16, :].astype(F32)
        dec, eta = scal[0:1] + scal[1:2], scal[2:3] + scal[3:4]
        hi, lo = split2(mem)
        a_mat = a_ref[h, 0:HD, :]
        mom = eta * mom - (mm(a_mat, hi) + mm(a_mat, lo)) + b_ref[h].astype(F32)
        return dec * mem + mom, mom

    tri = lax.broadcasted_iota(jnp.int32, (CR, CR), 1) <= lax.broadcasted_iota(jnp.int32, (CR, CR), 0)

    def attend(c):
        for h in range(2):
            q8 = qb[h, c * CR : (c + 1) * CR, :] * 8
            pv = mm(jnp.exp(mm_t(q8, pkb[h])).astype(BF16), pva[h])
            if c:
                w = jnp.exp(mm_t(q8, kb[h, 0 : c * CR, :])).astype(BF16)
                pv = pv + mm(w, va[h, 0 : c * CR, :])
            w = jnp.where(tri, jnp.exp(mm_t(q8, kb[h, c * CR : (c + 1) * CR, :])), 0.0)
            pv = pv + mm(w.astype(BF16), va[h, c * CR : (c + 1) * CR, :])
            attn[h, c * CR : (c + 1) * CR, :] = pv[:, :HD] / pv[:, HD:]

    attend(3)
    attend(2)
    if short:
        map_b(1).wait_recv()
        for h in range(2):
            first = st_b[0, h].astype(F32)
            mem, mom = advance(first, first, pk_a, pk_b, h)
            mid_out[h, 0] = mem.astype(BF16)
            mid_out[h, 1] = mom.astype(BF16)
        middle.start()
    attend(1)
    attend(0)

    w_xnb.wait_recv()
    w_fwd.start()

    if short:
        map_a(1).wait_recv()
        middle.wait_recv()
        carry = []
        for h in range(2):
            carry += advance(
                mid_in[h, 0].astype(F32), mid_in[h, 1].astype(F32), st_a.at[0], st_b.at[0], h
            )
    else:

        def chain(i, carry):
            d = span - 1 - i
            map_b(d).wait_recv()
            map_a(d).wait_recv()
            new = []
            for h in range(2):
                new += advance(carry[2 * h], carry[2 * h + 1], st_a.at[d - 1], st_b.at[d - 1], h)
            return tuple(new)

        carry = lax.fori_loop(0, span - 1, chain, (jnp.zeros((HD, HD), F32),) * 4)
    mats = [split2(carry[2 * h] * keep) for h in range(2)]

    for c in range(NC):
        for h in range(2):
            qh = qb[h, c * CR : (c + 1) * CR, :]
            retr = mm(qh, mats[h][0]) + mm(qh, mats[h][1])
            mem = retr * lax.rsqrt(jnp.mean(retr * retr, -1, keepdims=True) + EPS)
            hog[0, c, :, h * HD : (h + 1) * HD] = (
                attn[h, c * CR : (c + 1) * CR, :] + mem
            ).astype(BF16)
        h_xnb(c).start()
        h_sib(c).start()

    w_sib.wait_recv()
    w_fwd.wait_recv()
    for fetch in fetches[3:]:
        fetch.wait()

    def reduce_x(c):
        rs1(c).wait_recv()
        rs2_out[c] = (part2[c] + rs1_in[c, 1].astype(F32)).astype(BF16)
        rs2(c).start()
        part0[c] = part0[c] + rs1_in[c, 0].astype(F32)

    def ffn(c, _):
        h_xnb(c).wait_recv()
        h_fwd(c).start()
        h_sib(c).wait_recv()
        lhs = jnp.concatenate([hog[0, c], hog[1, c], hog[2, c]], 1)
        proj = mm(lhs, wog[0:3].reshape(3 * 256, d_model))
        h_fwd(c).wait_recv()
        projb[...] = proj + mm(hog[3, c], wog[3])
        sq = jnp.zeros((CR, 1), F32)
        for t in range(4):
            r = (xg[t, c].astype(F32) + projb[:, cols[t]]).astype(BF16)
            sq = sq + sumsq(r)
            resb[:, cols[t]] = r
        inv = lax.rsqrt(sq / d_model + EPS)

        @pl.when(c > 0)
        def _():
            reduce_x(c - 1)

        res = resb[...]
        gate = mm_t(res, wgate_ref[...]) * inv
        up = mm_t(res, wup_ref[...]) * inv
        hidden = (gate / (1.0 + jnp.exp(-gate)) * up).astype(BF16)
        rs1_out[c, 0] = mm(hidden, wdown_ref[:, cols[1]]).astype(BF16)
        rs1_out[c, 1] = mm(hidden, wdown_ref[:, cols[3]]).astype(BF16)
        rs1(c).start()
        part2[c] = mm(hidden, wdown_ref[:, cols[2]])
        part0[c] = mm(hidden, wdown_ref[:, cols[0]]) + resb[:, cols[0]].astype(F32)
        return 0

    lax.fori_loop(0, NC, ffn, 0)
    reduce_x(NC - 1)

    def last(c, _):
        rs2(c).wait_recv()
        out_ref[c] = (part0[c] + rs2_in[c].astype(F32)).astype(BF16)
        return 0

    lax.fori_loop(0, NC, last, 0)

    def drain(c, _):
        for copy in (x_sib, x_xnb, x_fwd, h_sib, h_xnb, h_fwd, rs1, rs2):
            copy(c).wait_send()
        return 0

    lax.fori_loop(0, NC, drain, 0)
    w_sib.wait_send()
    w_xnb.wait_send()
    w_fwd.wait_send()
    edge.wait_send()
    for d in range(1, direct):
        map_a(d).wait_send()
        map_b(d).wait_send()
    if short:
        middle.wait_send()


def body(n_seq, activations, seg_len, seg_start, memory_rates, w_qkv, conv_w, persistent, w_out, w_gate, w_up, w_down):
    span = n_seq // 2
    full = w_qkv.shape[0]
    hw = w_qkv.shape[2]
    ff = w_gate.shape[1]
    vmem = pl.BlockSpec(memory_space=pltpu.VMEM)
    hbm = pl.BlockSpec(memory_space=pl.ANY)
    smem = pl.BlockSpec(memory_space=pltpu.SMEM)
    dma = pltpu.SemaphoreType.DMA
    per_chunk = dma((NC,))
    out = pl.pallas_call(
        functools.partial(kernel, n_seq, span),
        out_shape=jax.ShapeDtypeStruct((NC, CR, hw), BF16),
        in_specs=[smem, smem, smem, hbm, hbm, vmem, vmem] + [hbm] * 4,
        out_specs=vmem,
        scratch_shapes=[
            pltpu.VMEM((4, NC, CR, hw), BF16),
            pltpu.VMEM((3, full, hw), BF16),
            pltpu.VMEM((ff, full), BF16),
            pltpu.VMEM((ff, full), BF16),
            pltpu.VMEM((ff, full), BF16),
            pltpu.VMEM((SEG + 8, 3 * hw), F32),
            pltpu.VMEM((8, 3 * hw), F32),
            pltpu.VMEM((8, 3 * hw), F32),
            pltpu.VMEM((2, SEG, HD), BF16),
            pltpu.VMEM((2, SEG, HD), BF16),
            pltpu.VMEM((2, SEG, 2 * HD), BF16),
            pltpu.VMEM((2, HD, HD), BF16),
            pltpu.VMEM((2, HD, 2 * HD), BF16),
            pltpu.VMEM((2, SEG, HD), F32),
            pltpu.VMEM((2, HD, 2 * HD), F32),
            pltpu.VMEM((2, HD + 16, HD), BF16),
            pltpu.VMEM((2, HD, HD), BF16),
            pltpu.VMEM((span - 1, 2, HD + 16, HD), BF16),
            pltpu.VMEM((span - 1, 2, HD, HD), BF16),
            pltpu.VMEM((2, 2, HD, HD), BF16),
            pltpu.VMEM((2, 2, HD, HD), BF16),
            pltpu.VMEM((CR, full), F32),
            pltpu.VMEM((CR, full), BF16),
            pltpu.VMEM((4, hw, full), BF16),
            pltpu.VMEM((4, NC, CR, hw), BF16),
            pltpu.VMEM((NC, CR, hw), F32),
            pltpu.VMEM((NC, CR, hw), F32),
            pltpu.VMEM((NC, 2, CR, hw), BF16),
            pltpu.VMEM((NC, 2, CR, hw), BF16),
            pltpu.VMEM((NC, CR, hw), BF16),
            pltpu.VMEM((NC, CR, hw), BF16),
        ]
        + [per_chunk] * 6
        + [dma((3,))] * 2
        + [per_chunk] * 6
        + [dma, dma]
        + [dma((span - 1,))] * 4
        + [dma, dma]
        + [per_chunk] * 4
        + [dma((6,))],
        compiler_params=pltpu.CompilerParams(
            collective_id=0, has_side_effects=True, vmem_limit_bytes=56 * 1024 * 1024
        ),
    )(
        seg_len,
        seg_start,
        memory_rates,
        activations.reshape(NC, CR, hw),
        jnp.transpose(w_qkv, (1, 0, 2)),
        jnp.transpose(conv_w, (1, 0, 2)),
        persistent,
        w_out,
        w_gate.T,
        w_up.T,
        w_down,
    )
    return out.reshape(SEG, hw)


def solution(mesh):
    return jax.shard_map(
        functools.partial(body, mesh.shape["seq"]),
        mesh=mesh,
        in_specs=(
            P("seq", ("tr", "tc")),
            P("seq"),
            P("seq"),
            P(None, "seq", None),
            P(None, None, ("tr", "tc")),
            P(None, None, ("tr", "tc")),
            P(None, None, ("tr", "tc")),
            P(("tr", "tc"), None),
            P(None, ("tr", "tc")),
            P(None, ("tr", "tc")),
            P(("tr", "tc"), None),
        ),
        out_specs=P("seq", ("tr", "tc")),
        check_vma=False,
    )
```

```python
import functools

import jax
import jax.numpy as jnp
from jax import lax
from jax.experimental import pallas as pl
from jax.experimental.pallas import tpu as pltpu
from jax.sharding import PartitionSpec as P

HD = 128
SEG = 1024
CONV = 4
NC = 4
CR = SEG // NC
EPS = 1e-06
MESH = pl.DeviceIdType.MESH
F32 = jnp.float32
BF16 = jnp.bfloat16


def mm(a, b):
    return jnp.dot(a, b, preferred_element_type=F32)


def mm_t(a, b):
    return lax.dot_general(a, b, (((1,), (1,)), ((), ())), preferred_element_type=F32)


def unit_rows(v):
    return v * lax.rsqrt(jnp.sum(v * v, -1, keepdims=True) + EPS)


def split2(v):
    hi = v.astype(BF16)
    return hi, (v - hi.astype(F32)).astype(BF16)


def kernel(
    n_seq,
    span,
    len_ref,
    start_ref,
    rates_ref,
    x_hbm,
    wqkv_hbm,
    conv_ref,
    pers_ref,
    wout_hbm,
    wgate_hbm,
    wup_hbm,
    wdown_hbm,
    out_ref,
    xg,
    wqkv_ref,
    wgate_ref,
    wup_ref,
    wdown_ref,
    ext,
    edge_out,
    edge_in,
    qb,
    kb,
    va,
    pkb,
    pva,
    attn,
    ab,
    pk_a,
    pk_b,
    st_a,
    st_b,
    mid_out,
    mid_in,
    projb,
    resb,
    wog,
    hog,
    part0,
    part2,
    rs1_out,
    rs1_in,
    rs2_out,
    rs2_in,
    xs_s, xs_r, xx_s, xx_r, xf_s, xf_r,
    ws_s, ws_r,
    hs_s, hs_r, hx_s, hx_r, hf_s, hf_r,
    ed_s, ed_r,
    sa_s, sa_r,
    sb_s, sb_r,
    md_s, md_r,
    r1_s, r1_r, r2_s, r2_r,
    lc_s,
):
    seq, tr, tc = lax.axis_index("seq"), lax.axis_index("tr"), lax.axis_index("tc")
    sib = (seq, tr, 1 - tc)
    xnb = (seq, 1 - tr, tc)
    d_model = 4 * 256
    group = (tr * 2 + tc, tr * 2 + 1 - tc, (1 - tr) * 2 + tc, (1 - tr) * 2 + 1 - tc)
    cols = [pl.ds(pl.multiple_of(g * 256, 256), 256) for g in group]

    def ahead(d):
        return (lax.rem(seq + d, n_seq), tr, tc)

    def send(src, dst, ssem, rsem, dev):
        return pltpu.make_async_remote_copy(
            src_ref=src, dst_ref=dst, send_sem=ssem, recv_sem=rsem, device_id=dev, device_id_type=MESH
        )

    fetches = [
        pltpu.make_async_copy(src, dst, lc_s.at[i])
        for i, (src, dst) in enumerate(
            (
                (x_hbm, xg.at[0]),
                (wqkv_hbm, wqkv_ref),
                (wout_hbm, wog.at[0]),
                (wgate_hbm, wgate_ref),
                (wup_hbm, wup_ref),
                (wdown_hbm, wdown_ref),
            )
        )
    ]
    for fetch in fetches:
        fetch.start()

    short = span == 4
    reach = 3 if short else span
    direct = 2 if short else span
    barrier = pltpu.get_barrier_semaphore()
    peers = [sib, xnb] + [ahead(d) for d in range(1, reach)] + [ahead(n_seq - d) for d in range(1, reach)]
    for peer in peers:
        pl.semaphore_signal(barrier, inc=1, device_id=peer, device_id_type=MESH)
    pl.semaphore_wait(barrier, len(peers))

    def x_sib(c):
        return send(x_hbm.at[c], xg.at[1, c], xs_s.at[c], xs_r.at[c], sib)

    def x_xnb(c):
        return send(x_hbm.at[c], xg.at[2, c], xx_s.at[c], xx_r.at[c], xnb)

    def x_fwd(c):
        return send(xg.at[2, c], xg.at[3, c], xf_s.at[c], xf_r.at[c], sib)

    def h_sib(c):
        return send(hog.at[0, c], hog.at[1, c], hs_s.at[c], hs_r.at[c], sib)

    def h_xnb(c):
        return send(hog.at[0, c], hog.at[2, c], hx_s.at[c], hx_r.at[c], xnb)

    def h_fwd(c):
        return send(hog.at[2, c], hog.at[3, c], hf_s.at[c], hf_r.at[c], sib)

    def rs1(c):
        return send(rs1_out.at[c], rs1_in.at[c], r1_s.at[c], r1_r.at[c], sib)

    def rs2(c):
        return send(rs2_out.at[c], rs2_in.at[c], r2_s.at[c], r2_r.at[c], xnb)

    w_sib = send(wog.at[0], wog.at[1], ws_s.at[0], ws_r.at[0], sib)
    half = pl.ds(pl.multiple_of(lax.rem(seq, 2) * 128, 128), 128)
    pair = (seq + 1 - 2 * lax.rem(seq, 2), tr, tc)
    w_xnb = send(wog.at[0, half], wog.at[2, half], ws_s.at[1], ws_r.at[1], xnb)
    w_pair = send(wog.at[2, half], wog.at[2, half], ws_s.at[3], ws_r.at[3], pair)
    w_fwd = send(wog.at[2], wog.at[3], ws_s.at[2], ws_r.at[2], sib)
    edge = send(edge_out, edge_in, ed_s, ed_r, ahead(1))

    def map_a(d):
        return send(pk_a, st_a.at[d - 1], sa_s.at[d - 1], sa_r.at[d - 1], ahead(d))

    def map_b(d):
        return send(pk_b, st_b.at[d - 1], sb_s.at[d - 1], sb_r.at[d - 1], ahead(d))

    middle = send(mid_out, mid_in, md_s, md_r, ahead(2)) if short else None

    order = (NC - 1,) + tuple(range(NC - 1))
    for c in order:
        x_xnb(c).start()
        x_sib(c).start()

    length = len_ref[0]
    continuing = start_ref[0] == 0
    keep = jnp.where(continuing, 1.0, 0.0).astype(F32)

    pkb[...] = jnp.zeros_like(pkb)
    pva[...] = jnp.zeros_like(pva)
    for h in range(2):
        lanes = slice(h * HD, (h + 1) * HD)
        pkb[h, 0:16, :] = unit_rows(pers_ref[0, :, lanes].astype(F32)).astype(BF16)
        pva[h, 0:16, 0:HD] = pers_ref[1, :, lanes]
        pva[h, 0:16, HD:] = jnp.ones((16, HD), BF16)

    def project(c, pair):
        lhs = [xg[t, c] for t in pair]
        return [
            sum(mm(x, wqkv_ref[p, cols[t], :]) for x, t in zip(lhs, pair)) for p in range(3)
        ]

    def rows8(c):
        return slice(8 + c * CR, 8 + (c + 1) * CR)

    fetches[0].wait()
    fetches[1].wait()
    for c in order:
        x_sib(c).wait_recv()
        for p, part in enumerate(project(c, (0, 1))):
            ext[rows8(c), p * 256 : (p + 1) * 256] = part

    def sumsq(v):
        v = v.astype(F32)
        return jnp.sum(v * v, -1, keepdims=True)

    def finish_projection(c):
        x_xnb(c).wait_recv()
        x_fwd(c).start()
        sq = sumsq(xg[0, c]) + sumsq(xg[1, c]) + sumsq(xg[2, c])
        x_fwd(c).wait_recv()
        inv = lax.rsqrt((sq + sumsq(xg[3, c])) / d_model + EPS)
        for p, part in enumerate(project(c, (2, 3))):
            lanes = slice(p * 256, (p + 1) * 256)
            ext[rows8(c), lanes] = ((ext[rows8(c), lanes] + part) * inv).astype(BF16).astype(F32)

    def conv_chunk(c):
        rows = slice(c * CR, (c + 1) * CR)
        live = (lax.broadcasted_iota(jnp.int32, (CR, HD), 0) + c * CR) < length
        for p in range(3):
            for h in range(2):
                lanes = slice(h * HD, (h + 1) * HD)
                slab = ext[c * CR : (c + 1) * CR + 8, p * 256 + h * HD : p * 256 + (h + 1) * HD]
                total = jnp.zeros((CR, HD), F32)
                for j in range(CONV):
                    total = total + conv_ref[p, j : j + 1, lanes] * slab[8 - j : 8 - j + CR, :]
                if p == 0:
                    qb[h, rows, :] = unit_rows(total).astype(BF16)
                elif p == 1:
                    kb[h, rows, :] = jnp.where(live, unit_rows(total), 0.0).astype(BF16)
                else:
                    va[h, rows, 0:HD] = jnp.where(live, total, 0.0).astype(BF16)
                    va[h, rows, HD:] = jnp.where(live, 1.0, 0.0).astype(BF16)
        for h in range(2):
            kh = kb[h, rows, :]
            both = jnp.concatenate([kh, va[h, rows, 0:HD]], 1)
            term = lax.dot_general(kh, both, (((0,), (0,)), ((), ())), preferred_element_type=F32)
            ab[h] = term if c == 0 else ab[h] + term

    finish_projection(NC - 1)
    edge_out[...] = ext[SEG : SEG + 8, :]
    edge.start()
    finish_projection(0)
    edge.wait_recv()
    ext[0:8, :] = edge_in[...] * keep
    conv_chunk(0)
    for c in range(1, NC - 1):
        finish_projection(c)
        if c == NC - 2:
            fetches[2].wait()
            w_xnb.start()
            w_sib.start()
        conv_chunk(c)
    conv_chunk(NC - 1)

    row = lax.broadcasted_iota(jnp.int32, (16, HD), 0)
    rates = [[rates_ref[k, 0, group[0] * 2 + h] for k in range(3)] for h in range(2)]
    for h in range(2):
        pk_b[h] = (ab[h, :, HD:] * rates[h][2]).astype(BF16)
    for d in range(direct - 1, 0, -1):
        map_b(d).start()
    for h in range(2):
        alpha, eta, theta = rates[h]
        pk_a[h, 0:HD, :] = (ab[h, :, 0:HD] * (theta * keep)).astype(BF16)
        d_hi, d_lo = split2(jnp.full((16, HD), (1.0 - alpha) * keep, F32))
        e_hi, e_lo = split2(jnp.full((16, HD), eta * keep, F32))
        pick = jnp.where(row == 0, d_hi.astype(F32), jnp.where(row == 1, d_lo.astype(F32), 0.0))
        pick = jnp.where(row == 2, e_hi.astype(F32), jnp.where(row == 3, e_lo.astype(F32), pick))
        pk_a[h, HD : HD + 16, :] = pick.astype(BF16)
    for d in range(direct - 1, 0, -1):
        map_a(d).start()

    def advance(mem, mom, a_ref, b_ref, h):
        scal = a_ref[h, HD : HD + 16, :].astype(F32)
        dec, eta = scal[0:1] + scal[1:2], scal[2:3] + scal[3:4]
        hi, lo = split2(mem)
        a_mat = a_ref[h, 0:HD, :]
        mom = eta * mom - (mm(a_mat, hi) + mm(a_mat, lo)) + b_ref[h].astype(F32)
        return dec * mem + mom, mom

    tri = lax.broadcasted_iota(jnp.int32, (CR, CR), 1) <= lax.broadcasted_iota(jnp.int32, (CR, CR), 0)

    def attend(c):
        for h in range(2):
            q8 = qb[h, c * CR : (c + 1) * CR, :] * 8
            pv = mm(jnp.exp(mm_t(q8, pkb[h])).astype(BF16), pva[h])
            if c:
                w = jnp.exp(mm_t(q8, kb[h, 0 : c * CR, :])).astype(BF16)
                pv = pv + mm(w, va[h, 0 : c * CR, :])
            w = jnp.where(tri, jnp.exp(mm_t(q8, kb[h, c * CR : (c + 1) * CR, :])), 0.0)
            pv = pv + mm(w.astype(BF16), va[h, c * CR : (c + 1) * CR, :])
            attn[h, c * CR : (c + 1) * CR, :] = pv[:, :HD] / pv[:, HD:]

    attend(3)
    attend(2)
    if short:
        map_b(1).wait_recv()
        for h in range(2):
            first = st_b[0, h].astype(F32)
            mem, mom = advance(first, first, pk_a, pk_b, h)
            mid_out[h, 0] = mem.astype(BF16)
            mid_out[h, 1] = mom.astype(BF16)
        middle.start()
    w_xnb.wait_recv()
    w_pair.start()
    attend(1)
    attend(0)


    if short:
        map_a(1).wait_recv()
        middle.wait_recv()
        carry = []
        for h in range(2):
            carry += advance(
                mid_in[h, 0].astype(F32), mid_in[h, 1].astype(F32), st_a.at[0], st_b.at[0], h
            )
    else:

        def chain(i, carry):
            d = span - 1 - i
            map_b(d).wait_recv()
            map_a(d).wait_recv()
            new = []
            for h in range(2):
                new += advance(carry[2 * h], carry[2 * h + 1], st_a.at[d - 1], st_b.at[d - 1], h)
            return tuple(new)

        carry = lax.fori_loop(0, span - 1, chain, (jnp.zeros((HD, HD), F32),) * 4)
    mats = [split2(carry[2 * h] * keep) for h in range(2)]

    for c in range(NC):
        for h in range(2):
            qh = qb[h, c * CR : (c + 1) * CR, :]
            retr = mm(qh, mats[h][0]) + mm(qh, mats[h][1])
            mem = retr * lax.rsqrt(jnp.mean(retr * retr, -1, keepdims=True) + EPS)
            hog[0, c, :, h * HD : (h + 1) * HD] = (
                attn[h, c * CR : (c + 1) * CR, :] + mem
            ).astype(BF16)
        h_xnb(c).start()
        h_sib(c).start()

    w_pair.wait_recv()
    w_fwd.start()
    w_sib.wait_recv()
    w_fwd.wait_recv()
    for fetch in fetches[3:]:
        fetch.wait()

    def reduce_x(c):
        rs1(c).wait_recv()
        rs2_out[c] = (part2[c] + rs1_in[c, 1].astype(F32)).astype(BF16)
        rs2(c).start()
        part0[c] = part0[c] + rs1_in[c, 0].astype(F32)

    def ffn(c, _):
        h_xnb(c).wait_recv()
        h_fwd(c).start()
        h_sib(c).wait_recv()
        lhs = jnp.concatenate([hog[0, c], hog[1, c], hog[2, c]], 1)
        proj = mm(lhs, wog[0:3].reshape(3 * 256, d_model))
        h_fwd(c).wait_recv()
        projb[...] = proj + mm(hog[3, c], wog[3])
        sq = jnp.zeros((CR, 1), F32)
        for t in range(4):
            r = (xg[t, c].astype(F32) + projb[:, cols[t]]).astype(BF16)
            sq = sq + sumsq(r)
            resb[:, cols[t]] = r
        inv = lax.rsqrt(sq / d_model + EPS)

        @pl.when(c > 0)
        def _():
            reduce_x(c - 1)

        res = resb[...]
        gate = mm_t(res, wgate_ref[...]) * inv
        up = mm_t(res, wup_ref[...]) * inv
        hidden = (gate / (1.0 + jnp.exp(-gate)) * up).astype(BF16)
        rs1_out[c, 0] = mm(hidden, wdown_ref[:, cols[1]]).astype(BF16)
        rs1_out[c, 1] = mm(hidden, wdown_ref[:, cols[3]]).astype(BF16)
        rs1(c).start()
        part2[c] = mm(hidden, wdown_ref[:, cols[2]])
        part0[c] = mm(hidden, wdown_ref[:, cols[0]]) + resb[:, cols[0]].astype(F32)
        return 0

    lax.fori_loop(0, NC, ffn, 0)
    reduce_x(NC - 1)

    def last(c, _):
        rs2(c).wait_recv()
        out_ref[c] = (part0[c] + rs2_in[c].astype(F32)).astype(BF16)
        return 0

    lax.fori_loop(0, NC, last, 0)

    def drain(c, _):
        for copy in (x_sib, x_xnb, x_fwd, h_sib, h_xnb, h_fwd, rs1, rs2):
            copy(c).wait_send()
        return 0

    lax.fori_loop(0, NC, drain, 0)
    w_sib.wait_send()
    w_xnb.wait_send()
    w_fwd.wait_send()
    w_pair.wait_send()
    edge.wait_send()
    for d in range(1, direct):
        map_a(d).wait_send()
        map_b(d).wait_send()
    if short:
        middle.wait_send()


def body(n_seq, activations, seg_len, seg_start, memory_rates, w_qkv, conv_w, persistent, w_out, w_gate, w_up, w_down):
    span = n_seq // 2
    full = w_qkv.shape[0]
    hw = w_qkv.shape[2]
    ff = w_gate.shape[1]
    vmem = pl.BlockSpec(memory_space=pltpu.VMEM)
    hbm = pl.BlockSpec(memory_space=pl.ANY)
    smem = pl.BlockSpec(memory_space=pltpu.SMEM)
    dma = pltpu.SemaphoreType.DMA
    per_chunk = dma((NC,))
    out = pl.pallas_call(
        functools.partial(kernel, n_seq, span),
        out_shape=jax.ShapeDtypeStruct((NC, CR, hw), BF16),
        in_specs=[smem, smem, smem, hbm, hbm, vmem, vmem] + [hbm] * 4,
        out_specs=vmem,
        scratch_shapes=[
            pltpu.VMEM((4, NC, CR, hw), BF16),
            pltpu.VMEM((3, full, hw), BF16),
            pltpu.VMEM((ff, full), BF16),
            pltpu.VMEM((ff, full), BF16),
            pltpu.VMEM((ff, full), BF16),
            pltpu.VMEM((SEG + 8, 3 * hw), F32),
            pltpu.VMEM((8, 3 * hw), F32),
            pltpu.VMEM((8, 3 * hw), F32),
            pltpu.VMEM((2, SEG, HD), BF16),
            pltpu.VMEM((2, SEG, HD), BF16),
            pltpu.VMEM((2, SEG, 2 * HD), BF16),
            pltpu.VMEM((2, HD, HD), BF16),
            pltpu.VMEM((2, HD, 2 * HD), BF16),
            pltpu.VMEM((2, SEG, HD), F32),
            pltpu.VMEM((2, HD, 2 * HD), F32),
            pltpu.VMEM((2, HD + 16, HD), BF16),
            pltpu.VMEM((2, HD, HD), BF16),
            pltpu.VMEM((span - 1, 2, HD + 16, HD), BF16),
            pltpu.VMEM((span - 1, 2, HD, HD), BF16),
            pltpu.VMEM((2, 2, HD, HD), BF16),
            pltpu.VMEM((2, 2, HD, HD), BF16),
            pltpu.VMEM((CR, full), F32),
            pltpu.VMEM((CR, full), BF16),
            pltpu.VMEM((4, hw, full), BF16),
            pltpu.VMEM((4, NC, CR, hw), BF16),
            pltpu.VMEM((NC, CR, hw), F32),
            pltpu.VMEM((NC, CR, hw), F32),
            pltpu.VMEM((NC, 2, CR, hw), BF16),
            pltpu.VMEM((NC, 2, CR, hw), BF16),
            pltpu.VMEM((NC, CR, hw), BF16),
            pltpu.VMEM((NC, CR, hw), BF16),
        ]
        + [per_chunk] * 6
        + [dma((4,))] * 2
        + [per_chunk] * 6
        + [dma, dma]
        + [dma((span - 1,))] * 4
        + [dma, dma]
        + [per_chunk] * 4
        + [dma((6,))],
        compiler_params=pltpu.CompilerParams(
            collective_id=0, has_side_effects=True, vmem_limit_bytes=56 * 1024 * 1024
        ),
    )(
        seg_len,
        seg_start,
        memory_rates,
        activations.reshape(NC, CR, hw),
        jnp.transpose(w_qkv, (1, 0, 2)),
        jnp.transpose(conv_w, (1, 0, 2)),
        persistent,
        w_out,
        w_gate.T,
        w_up.T,
        w_down,
    )
    return out.reshape(SEG, hw)


def solution(mesh):
    return jax.shard_map(
        functools.partial(body, mesh.shape["seq"]),
        mesh=mesh,
        in_specs=(
            P("seq", ("tr", "tc")),
            P("seq"),
            P("seq"),
            P(None, "seq", None),
            P(None, None, ("tr", "tc")),
            P(None, None, ("tr", "tc")),
            P(None, None, ("tr", "tc")),
            P(("tr", "tc"), None),
            P(None, ("tr", "tc")),
            P(None, ("tr", "tc")),
            P(("tr", "tc"), None),
        ),
        out_specs=P("seq", ("tr", "tc")),
        check_vma=False,
    )
```
